128 devices in a mesh: dp: 8 (over x, y_lo), feat: 16 (over z, y_hi, core).
Axes of the slice: x: 4, y: 4 (y_hi: 2, y_lo: 2; y = y_hi * 2 + y_lo), z: 4, core: 2. Of those that a mesh axis runs over, the one named last changes fastest.
Arguments:
- view_a: float32 [8192, 4096], P('dp', 'feat'), may hold values from -1000 to 1000
- view_b: float32 [8192, 4096], P('dp', 'feat'), may hold values from -1000 to 1000
Outputs:
- grad_a: float32 [8192, 4096], P('dp', 'feat')
- grad_b: float32 [8192, 4096], P('dp', 'feat')
- loss: float32 [], replicated
The draws below stay inside these ranges and needn't reach their ends.
All inputs are finite; a program needn't handle non-finite values.
Results may differ from the reference program's by a relative error of at most 0.0017.
Values may be sent and summed in bfloat16 or wider, within the bound.
A program may use at most 128 MiB of HBM per device.

```python
import jax
import jax.numpy as jnp
from jax import lax

D = 4096
BATCH = 8192


def shared_parts(key):
    keys = jax.random.split(key, 4)
    groups = max(D // 64, 1)
    normal_base = jnp.clip(jax.random.normal(keys[0], (BATCH, D), jnp.float32), -4.0, 4.0)
    base = normal_base
    latent = jnp.clip(jax.random.normal(keys[2], (BATCH, groups), jnp.float32), -4.0, 4.0)
    member = jax.random.randint(keys[3], (D,), 0, groups)
    position = lax.broadcasted_iota(jnp.int32, (BATCH,), 0).astype(jnp.float32) / BATCH
    row_scale = jnp.exp(jnp.log(3.0) * position)
    return row_scale[:, None] * (base + jnp.take(latent, member, axis=1))


def view_from(key, common):
    keys = jax.random.split(key, 4)
    normal_noise = jnp.clip(jax.random.normal(keys[0], (BATCH, D), jnp.float32), -4.0, 4.0)
    noise = normal_noise
    column_scale = jnp.exp(jax.random.uniform(keys[2], (D,), jnp.float32, 0.0, jnp.log(10.0)))
    offset = jax.random.uniform(keys[3], (D,), jnp.float32, -2.0, 2.0)
    return column_scale * (offset + common + 0.5 * noise)


def draw_view_a(key, part):
    common = shared_parts(key)
    key = jax.random.fold_in(key, 11)
    return view_from(key, common)


def draw_view_b(key, part):
    common = shared_parts(key)
    key = jax.random.fold_in(key, 23)
    return view_from(key, common)


def setup_inputs(seed: int = 0) -> dict:
    splits = jax.random.split(jax.random.key(seed), 3)
    return {
        "view_a": draw_view_a(jax.random.fold_in(splits[2], 71), 0),
        "view_b": draw_view_b(jax.random.fold_in(splits[2], 71), 0),
    }


off_weight = 0.0051
variance_eps = 1e-05

def standardize(view):
    center = lax.optimization_barrier(jnp.mean(view, axis=0))
    shifted = view - center
    spread = jnp.sqrt(lax.optimization_barrier(jnp.mean(shifted * shifted, axis=0)) + variance_eps)
    return (shifted / spread, spread)

def backward(upstream, normed, spread):
    first = lax.optimization_barrier(jnp.mean(upstream, axis=0))
    second = lax.optimization_barrier(jnp.mean(upstream * normed, axis=0))
    return (upstream - first - normed * second) / spread

def reference(view_a, view_b):
    normed_a, spread_a = standardize(view_a)
    normed_b, spread_b = standardize(view_b)
    half_a = normed_a.astype(jnp.bfloat16)
    half_b = normed_b.astype(jnp.bfloat16)
    correlation = jnp.dot(half_a.T, half_b, preferred_element_type=jnp.float32) / BATCH
    columns = correlation.shape[0]
    on_diagonal = lax.broadcasted_iota(jnp.int32, (columns, columns), 0) == lax.broadcasted_iota(jnp.int32, (columns, columns), 1)
    diagonal = jnp.diagonal(correlation)
    total_loss = (jnp.sum((1.0 - diagonal) ** 2) + off_weight * (jnp.sum(correlation * correlation) - jnp.sum(diagonal * diagonal))) / D
    weights = jnp.where(on_diagonal, -2.0 * (1.0 - correlation), 2.0 * off_weight * correlation).astype(jnp.bfloat16)
    upstream_a = jnp.dot(half_b, weights.T, preferred_element_type=jnp.float32)
    upstream_b = jnp.dot(half_a, weights, preferred_element_type=jnp.float32)
    grad_a = backward(upstream_a, normed_a, spread_a)
    grad_b = backward(upstream_b, normed_b, spread_b)
    return (grad_a, grad_b, total_loss)
```

```python
import functools

import jax
import jax.numpy as jnp
from jax import lax
from jax.experimental import pallas as pl
from jax.experimental.pallas import tpu as pltpu
from jax.sharding import PartitionSpec as P

D = 4096
BATCH = 8192
ROWS = 1024
COLS = 256
WIDE = 4 * COLS
EXTRA = 16
OWNED = COLS // 8

off_weight = 0.0051
variance_eps = 1e-05
scale_off = 2.0 * off_weight / BATCH

MESH = pl.DeviceIdType.MESH
BF16 = jnp.bfloat16
F32 = jnp.float32
VMEM = pltpu.VMEM
DMA = pltpu.SemaphoreType.DMA


def flip(index, mask):
    for bit in (1, 2, 4, 8):
        if mask & bit:
            index = index + bit - 2 * bit * ((index // bit) % 2)
    return index


def tree_sum(terms):
    while len(terms) > 1:
        terms = [terms[i] + terms[i + 1] for i in range(0, len(terms), 2)]
    return terms[0]


def matmul(a, b, contract):
    return lax.dot_general(a, b, (contract, ((), ())), preferred_element_type=F32)


def column_sum(value):
    return jnp.sum(value, axis=0, keepdims=True)


def kernel(
    va, vb, ga, gb, loss,
    stat, mid, sums_a, sums_b, vec_a, vec_b, vec_l,
    a_buf, b_buf, bt, corr, c_send, c_recv, w_buf,
    ua_acc, ub_own, ua_near, ua_send, ua_recv, ub_send, ub_recv, second_acc,
    stat_s, stat_r, mid_s, mid_r, sum_s, sum_r, vec_s, vec_r, vl_s, vl_r,
    a_s, a_r, b_s, b_r, c_s, c_r, w_s, w_r, ua_s, ua_r, ub_s, ub_r,
):
    p = lax.axis_index("dp")
    f = lax.axis_index("feat")
    dp_peer = [(flip(p, r), f) for r in range(8)]
    j_peer = [(p, flip(f, r)) for r in range(4)]
    z_peer = [(p, flip(f, 4 * r)) for r in range(4)]
    pending = []

    def copy(src, dst, send_sem, recv_sem, peer):
        return pltpu.make_async_remote_copy(
            src_ref=src, dst_ref=dst, send_sem=send_sem, recv_sem=recv_sem,
            device_id=peer, device_id_type=MESH,
        )

    def start(*args):
        handle = copy(*args)
        handle.start()
        pending.append(handle)
        return handle

    barrier = pltpu.get_barrier_semaphore()
    for peer in dp_peer[1:] + j_peer[1:] + z_peer[1:]:
        pl.semaphore_signal(barrier, inc=1, device_id=peer, device_id_type=MESH)

    zero_row = jnp.zeros((1, COLS), F32)
    mean_a = column_sum(va[...]) / ROWS
    mean_b = column_sum(vb[...]) / ROWS
    square_a = column_sum((va[...] - mean_a) ** 2)
    square_b = column_sum((vb[...] - mean_b) ** 2)
    stat[0] = jnp.concatenate([mean_a, square_a, mean_b, square_b] + [zero_row] * 4, axis=0)
    pl.semaphore_wait(barrier, 13)
    arrive = [start(stat.at[0], stat.at[r], stat_s.at[r], stat_r.at[r], dp_peer[r]) for r in range(1, 8)]
    for handle in arrive:
        handle.wait_recv()
    every = [stat[r] for r in range(8)]
    mean = tree_sum(every) / 8
    spreads = tree_sum([(t - mean) ** 2 for t in every]) * ROWS
    squares = tree_sum(every)
    center_a, center_b = mean[0:1], mean[2:3]
    spread_a = jnp.sqrt((squares[1:2] + spreads[0:1]) / BATCH + variance_eps)
    spread_b = jnp.sqrt((squares[3:4] + spreads[2:3]) / BATCH + variance_eps)
    inverse_a, inverse_b = 1.0 / spread_a, 1.0 / spread_b

    b_buf[0, 0:ROWS] = ((vb[...] - center_b) * inverse_b).astype(BF16)
    b_near = [
        start(b_buf.at[0, pl.ds(0, ROWS)], b_buf.at[r, pl.ds(0, ROWS)], b_s.at[r], b_r.at[r], z_peer[r])
        for r in (1, 3)
    ]
    pending = pending[:-2]
    a_buf[0, 0:ROWS] = ((va[...] - center_a) * inverse_a).astype(BF16)
    a_near = [start(a_buf.at[0, pl.ds(0, ROWS)], a_buf.at[r, pl.ds(0, ROWS)], a_s.at[r], a_r.at[r], j_peer[r]) for r in (2, 1)]
    half_a = a_buf[0, 0:ROWS].astype(F32)
    half_b = b_buf[0, 0:ROWS].astype(F32)
    mid[0] = jnp.concatenate(
        [column_sum(half_a * half_b), column_sum(half_a), column_sum(half_b)] + [zero_row] * 5, axis=0
    )
    mid_arrive = [start(mid.at[0], mid.at[r], mid_s.at[r], mid_r.at[r], dp_peer[r]) for r in range(1, 8)]
    bt[...] = b_buf[0, 0:ROWS].T
    for handle in mid_arrive:
        handle.wait_recv()
    totals = tree_sum([mid[r] for r in range(8)])
    sums_a[0] = totals
    sums_b[0] = totals
    sum_arrive = [start(sums_a.at[0], sums_a.at[r], sum_s.at[r], sum_r.at[r], j_peer[r]) for r in range(1, 4)]
    sum_arrive += [start(sums_b.at[0], sums_b.at[r], sum_s.at[3 + r], sum_r.at[3 + r], z_peer[r]) for r in range(1, 4)]
    diagonal = totals[0:1] / BATCH
    diag_weight = (-2.0 * (1.0 - diagonal)).astype(BF16).astype(F32)

    def correlate(k, m):
        block = matmul(bt[...], a_buf[m, 0:ROWS], ((1,), (0,)))
        if k == 0 and m == 0:
            same = lax.broadcasted_iota(jnp.int32, block.shape, 0) == lax.broadcasted_iota(jnp.int32, block.shape, 1)
            block = jnp.where(same, 0.0, block)
        corr[k, :, m * COLS : (m + 1) * COLS] = block
        c_send[k, :, m * COLS : (m + 1) * COLS] = block.astype(BF16)

    def scatter(k):
        got = []
        for r in range(1, 8):
            rows = pl.ds(pl.multiple_of(dp_peer[r][0] * OWNED, OWNED), OWNED)
            got.append(start(c_send.at[k, rows], c_recv.at[k, r], c_s.at[k, r], c_r.at[k, r], dp_peer[r]))
        return got

    own_rows = pl.ds(pl.multiple_of(p * OWNED, OWNED), OWNED)

    def reduce(k, got):
        for handle in got:
            handle.wait_recv()
        total = tree_sum([corr[k, own_rows, :]] + [c_recv[k, r].astype(F32) for r in range(1, 8)])
        w_buf[k, own_rows, :] = (total * scale_off).astype(BF16)
        part = w_buf.at[k, own_rows]
        return [start(part, part, w_s.at[k, r], w_r.at[k, r], dp_peer[r]) for r in range(1, 8)]

    correlate(0, 0)
    a_near[1].wait_recv()
    correlate(0, 1)
    a_near[0].wait_recv()
    a_far = start(a_buf.at[2, pl.ds(0, ROWS)], a_buf.at[3, pl.ds(0, ROWS)], a_s.at[3], a_r.at[3], j_peer[1])
    correlate(0, 2)
    a_far.wait_recv()
    correlate(0, 3)
    parts = {0: scatter(0)}
    for handle in b_near:
        handle.wait_send()
    b_far = start(b_buf.at[0, pl.ds(0, ROWS)], b_buf.at[2, pl.ds(0, ROWS)], b_s.at[2], b_r.at[2], z_peer[2])
    weights = {}
    for k, handle in ((1, b_near[0]), (3, b_near[1]), (2, b_far)):
        handle.wait_recv()
        bt[...] = b_buf[k, 0:ROWS].T
        for m in range(4):
            correlate(k, m)
        parts[k] = scatter(k)
        if k == 3:
            weights[0] = reduce(0, parts[0])
    for handle in sum_arrive:
        handle.wait_recv()
    for r in range(4):
        for sums, row, buf in ((sums_a, 1, a_buf), (sums_b, 2, b_buf)):
            value = sums[r, row : row + 1]
            high = value.astype(BF16)
            low = (value - high.astype(F32)).astype(BF16)
            buf[r, ROWS : ROWS + EXTRA] = jnp.concatenate(
                [high.astype(F32), low.astype(F32), jnp.zeros((EXTRA - 2, COLS), F32)], axis=0
            ).astype(BF16)
    for k in (1, 3, 2):
        weights[k] = reduce(k, parts[k])

    ub_arrive = {}
    vecb_arrive = {}
    for n, k in enumerate((0, 1, 3, 2)):
        for handle in weights[k]:
            handle.wait_recv()
        total = None
        for m in range(4):
            w = w_buf[k, :, m * COLS : (m + 1) * COLS]
            term = matmul(a_buf[m], w, ((1,), (1,)))
            total = term if total is None else total + term
        if k == 0:
            ub_own[...] = total[0:ROWS]
        else:
            ub_send[k] = total[0:ROWS].astype(BF16)
            ub_arrive[k] = start(ub_send.at[k], ub_recv.at[k], ub_s.at[k], ub_r.at[k], z_peer[k])
        square = jnp.square(w_buf[k].astype(F32))
        over_second = column_sum(square)
        folded = sum(square[:, i * 128 : (i + 1) * 128] for i in range(8))
        over_first = column_sum(folded.T)
        first = total[ROWS : ROWS + 1] + total[ROWS + 1 : ROWS + 2]
        slot = vec_b.at[0 if k == 0 else 3 + k]
        slot[...] = jnp.concatenate([first, over_first] + [zero_row] * 6, axis=0)
        if k:
            vecb_arrive[k] = start(slot, vec_b.at[k], vec_s.at[3 + k], vec_r.at[3 + k], z_peer[k])
        if n == 0:
            second_acc[0:1] = over_second
        else:
            second_acc[0:1] += over_second
        for m in range(4):
            w = w_buf[k, :, m * COLS : (m + 1) * COLS]
            term = matmul(b_buf[k], w, ((1,), (0,)))
            if n == 0:
                ua_acc[m] = term
            else:
                ua_acc[m] += term
    ua3 = start(ua_acc.at[3, pl.ds(0, ROWS)], ua_near.at[1], ua_s.at[3], ua_r.at[3], j_peer[1])
    ua1 = start(ua_acc.at[1, pl.ds(0, ROWS)], ua_near.at[0], ua_s.at[1], ua_r.at[1], j_peer[1])

    block_sum = sum(second_acc[0:1, m * COLS : (m + 1) * COLS] for m in range(4))
    loss_row = (1.0 - diagonal) ** 2 + (0.25 / off_weight) * block_sum
    vec_arrive = []
    for r in range(4):
        first = ua_acc[r, ROWS : ROWS + 1] + ua_acc[r, ROWS + 1 : ROWS + 2]
        second = second_acc[0:1, r * COLS : (r + 1) * COLS]
        slot = vec_a.at[0 if r == 0 else 3 + r]
        slot[...] = jnp.concatenate([first, second, loss_row] + [zero_row] * 5, axis=0)
        if r:
            vec_arrive.append(start(slot, vec_a.at[r], vec_s.at[r], vec_r.at[r], j_peer[r]))
    ua3.wait_recv()
    ua_send[...] = (ua_acc[2, 0:ROWS] + ua_near[1]).astype(BF16)
    ua2 = start(ua_send, ua_recv, ua_s.at[2], ua_r.at[2], j_peer[2])
    for handle in vec_arrive:
        handle.wait_recv()
    sum_a = tree_sum([vec_a[r] for r in range(4)])
    vec_l[0] = sum_a
    loss_arrive = [start(vec_l.at[0], vec_l.at[r], vl_s.at[r], vl_r.at[r], z_peer[r]) for r in range(1, 4)]
    for handle in vecb_arrive.values():
        handle.wait_recv()
    sum_b = tree_sum([vec_b[r] for r in range(4)])
    for handle in loss_arrive:
        handle.wait_recv()
    losses = tree_sum([vec_l[r] for r in range(4)])
    loss[...] = jnp.sum(losses[2:3], axis=1, keepdims=True) / D

    def finish(upstream, view, center, inverse, own_sum, sums, out):
        first = (sums[0:1] + diag_weight * own_sum) / BATCH
        second = sums[1:2] * (0.5 / off_weight) + diag_weight * diagonal
        normed = (view[...] - center) * inverse
        out[...] = (upstream - first - normed * second) * inverse

    for k in (1, 3, 2):
        ub_arrive[k].wait_recv()
    upstream_b = ub_own[...] + sum(ub_recv[k].astype(F32) for k in (1, 2, 3)) + diag_weight * a_buf[0, 0:ROWS].astype(F32)
    finish(upstream_b, vb, center_b, inverse_b, totals[1:2], sum_b, gb)
    ua1.wait_recv()
    ua2.wait_recv()
    upstream_a = ua_acc[0, 0:ROWS] + ua_near[0] + ua_recv[...].astype(F32) + diag_weight * b_buf[0, 0:ROWS].astype(F32)
    finish(upstream_a, va, center_a, inverse_a, totals[2:3], sum_a, ga)

    for handle in pending:
        handle.wait_send()


def per_device(view_a, view_b):
    small = VMEM((8, 8, COLS), F32)
    block = VMEM((4, ROWS + EXTRA, COLS), BF16)
    plain = VMEM((4, ROWS, COLS), BF16)
    chunk = (4, COLS, WIDE)
    grad_a, grad_b, loss = pl.pallas_call(
        kernel,
        out_shape=(
            jax.ShapeDtypeStruct((ROWS, COLS), F32),
            jax.ShapeDtypeStruct((ROWS, COLS), F32),
            jax.ShapeDtypeStruct((1, 1), F32),
        ),
        in_specs=[pl.BlockSpec(memory_space=VMEM)] * 2,
        out_specs=[pl.BlockSpec(memory_space=VMEM)] * 3,
        scratch_shapes=[
            small, small, small, small, small, small, small,
            block, block, VMEM((COLS, ROWS), BF16), VMEM(chunk, F32), VMEM(chunk, BF16),
            VMEM((4, 8, OWNED, WIDE), BF16), VMEM(chunk, BF16),
            VMEM((4, ROWS + EXTRA, COLS), F32), VMEM((ROWS, COLS), F32),
            VMEM((2, ROWS, COLS), F32), VMEM((ROWS, COLS), BF16), VMEM((ROWS, COLS), BF16), plain, plain, VMEM((8, WIDE), F32),
            DMA((8,)), DMA((8,)), DMA((8,)), DMA((8,)), DMA((8,)), DMA((8,)), DMA((8,)), DMA((8,)), DMA((4,)), DMA((4,)),
            DMA((4,)), DMA((4,)), DMA((4,)), DMA((4,)), DMA((4, 8)), DMA((4, 8)), DMA((4, 8)), DMA((4, 8)),
            DMA((4,)), DMA((4,)), DMA((4,)), DMA((4,)),
        ],
        compiler_params=pltpu.CompilerParams(
            collective_id=0, has_side_effects=True, vmem_limit_bytes=56 * 1024 * 1024
        ),
        cost_estimate=pl.CostEstimate(flops=3 * 2 * 1024**3, bytes_accessed=4 * 1024 * 1024, transcendentals=0),
        name="twins",
    )(view_a, view_b)
    return grad_a, grad_b, loss[0, 0]


def solution(mesh):
    in_specs = (P("dp", "feat"), P("dp", "feat"))
    out_specs = (P("dp", "feat"), P("dp", "feat"), P())
    return jax.shard_map(
        per_device, mesh=mesh, in_specs=in_specs, out_specs=out_specs, check_vma=False
    )
```

```python
import functools

import jax
import jax.numpy as jnp
from jax import lax
from jax.experimental import pallas as pl
from jax.experimental.pallas import tpu as pltpu
from jax.sharding import PartitionSpec as P

D = 4096
BATCH = 8192
ROWS = 1024
COLS = 256
WIDE = 4 * COLS
EXTRA = 16
OWNED = COLS // 8

off_weight = 0.0051
variance_eps = 1e-05
scale_off = 2.0 * off_weight / BATCH
along = 0.5 / off_weight

MESH = pl.DeviceIdType.MESH
BF16 = jnp.bfloat16
F32 = jnp.float32
VMEM = pltpu.VMEM
DMA = pltpu.SemaphoreType.DMA


def flip(index, mask):
    for bit in (1, 2, 4, 8):
        if mask & bit:
            index = index + bit - 2 * bit * ((index // bit) % 2)
    return index


def tree_sum(terms):
    while len(terms) > 1:
        terms = [terms[i] + terms[i + 1] for i in range(0, len(terms), 2)]
    return terms[0]


def matmul(a, b, contract):
    return lax.dot_general(a, b, (contract, ((), ())), preferred_element_type=F32)


def column_sum(value):
    return jnp.sum(value, axis=0, keepdims=True)


def kernel(
    va_hbm, vb_hbm, ga, gb, loss,
    va, vb,
    stat, mid, sums_a, sums_b, vec_a, vec_b, vec_l,
    coef_j, coef_z, a_raw, b_raw, a_buf, b_buf, bt, corr, c_send, c_relay, c_right, c_left, c_cross, w_buf,
    ua_acc, ub_own, ua_near, ua_send, ua_recv, ub_send, ub_recv, second_acc,
    io, stat_s, stat_r, mid_s, mid_r, sum_s, sum_r, vec_s, vec_r, vl_s, vl_r,
    coef_s, coef_r, a_s, a_r, b_s, b_r, c_s, c_r, w_s, w_r, ua_s, ua_r, ub_s, ub_r,
):
    p = lax.axis_index("dp")
    f = lax.axis_index("feat")
    across = p // 2
    side = p % 2
    dp_peer = [(flip(p, r), f) for r in range(8)]
    j_peer = [(p, flip(f, r)) for r in range(4)]
    z_peer = [(p, flip(f, 4 * r)) for r in range(4)]
    pending = []

    def start(src, dst, send_sem, recv_sem, peer):
        handle = pltpu.make_async_remote_copy(
            src_ref=src, dst_ref=dst, send_sem=send_sem, recv_sem=recv_sem,
            device_id=peer, device_id_type=MESH,
        )
        handle.start()
        pending.append(handle)
        return handle

    barrier = pltpu.get_barrier_semaphore()
    for peer in dp_peer[1:] + j_peer[1:] + z_peer[1:]:
        pl.semaphore_signal(barrier, inc=1, device_id=peer, device_id_type=MESH)
    load_a = pltpu.make_async_copy(va_hbm, va, io.at[0])
    load_b = pltpu.make_async_copy(vb_hbm, vb, io.at[1])
    load_a.start()
    load_b.start()

    zero_row = jnp.zeros((1, COLS), F32)
    load_a.wait()
    mean_a = column_sum(va[...]) / ROWS
    square_a = column_sum((va[...] - mean_a) ** 2)
    load_b.wait()
    mean_b = column_sum(vb[...]) / ROWS
    square_b = column_sum((vb[...] - mean_b) ** 2)
    stat[0] = jnp.concatenate([mean_a, square_a, mean_b, square_b] + [zero_row] * 4, axis=0)
    local_a = jnp.sqrt(square_a / ROWS + variance_eps)
    local_b = jnp.sqrt(square_b / ROWS + variance_eps)
    whole = pl.ds(0, ROWS)
    a_raw[0] = ((va[...] - mean_a) * (1.0 / local_a)).astype(BF16)
    b_raw[0] = ((vb[...] - mean_b) * (1.0 / local_b)).astype(BF16)
    pl.semaphore_wait(barrier, 13)
    arrive = [start(stat.at[0], stat.at[r], stat_s.at[r], stat_r.at[r], dp_peer[r]) for r in range(1, 8)]
    b_near = {r: start(b_raw.at[0], b_raw.at[r], b_s.at[r], b_r.at[r], z_peer[r]) for r in (1, 3)}
    a_near = {r: start(a_raw.at[0], a_raw.at[r], a_s.at[r], a_r.at[r], j_peer[r]) for r in (1, 2)}
    for handle in arrive:
        handle.wait_recv()
    every = [stat[r] for r in range(8)]
    mean = tree_sum(every) / 8
    spreads = tree_sum([(t - mean) ** 2 for t in every]) * ROWS
    squares = tree_sum(every)
    center_a, center_b = mean[0:1], mean[2:3]
    spread_a = jnp.sqrt((squares[1:2] + spreads[0:1]) / BATCH + variance_eps)
    spread_b = jnp.sqrt((squares[3:4] + spreads[2:3]) / BATCH + variance_eps)
    inverse_a, inverse_b = 1.0 / spread_a, 1.0 / spread_b
    coef_j[0] = jnp.concatenate([local_a * inverse_a, (mean_a - center_a) * inverse_a] + [zero_row] * 6, axis=0)
    coef_z[0] = jnp.concatenate([local_b * inverse_b, (mean_b - center_b) * inverse_b] + [zero_row] * 6, axis=0)
    coef_arrive = {}
    for n, (coef, peers) in enumerate(((coef_j, j_peer), (coef_z, z_peer))):
        for r in range(1, 4):
            coef_arrive[n, r] = start(coef.at[0], coef.at[r], coef_s.at[4 * n + r], coef_r.at[4 * n + r], peers[r])

    def half_of(view, center, inverse):
        return ((view[...] - center) * inverse).astype(BF16).astype(F32)

    def rescale_a(r):
        if r:
            coef_arrive[0, r].wait_recv()
        a_buf[r, 0:ROWS] = (a_raw[r].astype(F32) * coef_j[r, 0:1] + coef_j[r, 1:2]).astype(BF16)

    def rescale_b(r):
        if r:
            coef_arrive[1, r].wait_recv()
        b_buf[r, 0:ROWS] = (b_raw[r].astype(F32) * coef_z[r, 0:1] + coef_z[r, 1:2]).astype(BF16)
        bt[r] = b_buf[r, 0:ROWS].T

    def correlate(k, m):
        block = matmul(bt[k], a_buf[m, 0:ROWS], ((1,), (0,)))
        if k == 0 and m == 0:
            same = lax.broadcasted_iota(jnp.int32, block.shape, 0) == lax.broadcasted_iota(jnp.int32, block.shape, 1)
            block = jnp.where(same, 0.0, block)
        corr[k, :, m * COLS : (m + 1) * COLS] = block
        c_send[k, :, m * COLS : (m + 1) * COLS] = block.astype(BF16)

    units = [
        (0, 0, WIDE // 2, "x"), (1, 0, WIDE, "x"), (3, 0, WIDE, "y"), (2, 0, WIDE, "x"), (0, WIDE // 2, WIDE // 2, "y"),
    ]
    right, opposite, left = (flip(across, r) for r in (1, 2, 3))
    to_right, to_left, to_mate = dp_peer[2], dp_peer[6], dp_peer[1]

    def rows_at(first, count):
        return pl.ds(pl.multiple_of(first, 16), count)

    def layout(order):
        if order == "x":
            return (lambda x: 2 * OWNED * x), 2 * OWNED
        return (lambda x: 4 * OWNED * side + OWNED * x), OWNED

    def own_rows(order, whose):
        first = 2 * OWNED * across + OWNED * whose if order == "x" else 4 * OWNED * whose + OWNED * across
        return rows_at(first, OWNED)

    near, relays, crossed = {}, {}, {}

    def send_sum(u, first, count, dst, slot, peer):
        k, c0, width, _ = units[u]
        cols = pl.ds(c0, width)
        return start(c_send.at[k, rows_at(first, count), cols], dst.at[k, :, cols], c_s.at[u, slot], c_r.at[u, slot], peer)

    def send_along_x(u):
        base, count = layout(units[u][3])
        half = count // 2
        k, c0, width, _ = units[u]
        cols = pl.ds(c0, width)

        def part(x, which, dst, slot, peer):
            return start(
                c_send.at[k, rows_at(base(x) + which * half, half), cols],
                dst.at[k, pl.ds(which * half, half), cols], c_s.at[u, slot], c_r.at[u, slot], peer,
            )

        relays[u] = [part(opposite, 0, c_relay, 0, to_right), part(opposite, 1, c_relay, 1, to_left)]
        near[u] = [part(right, 0, c_right, 2, to_right), part(left, 1, c_left, 3, to_left)]

    def relay(u):
        k, c0, width, order = units[u]
        base, count = layout(order)
        half = count // 2
        cols = slice(c0, c0 + width)
        ends = ((0, left, c_left, 4, to_left), (1, right, c_right, 5, to_right))
        for which, x, dst, slot, peer in ends:
            relays[u][which].wait_recv()
            rows = rows_at(base(x) + which * half, half)
            got = c_relay[k, which * half : (which + 1) * half, cols].astype(F32)
            c_send[k, rows, cols] = (corr[k, rows, cols] + got).astype(BF16)
            near[u].append(
                start(
                    c_send.at[k, rows, pl.ds(c0, width)], dst.at[k, pl.ds(which * half, half), pl.ds(c0, width)],
                    c_s.at[u, slot], c_r.at[u, slot], peer,
                )
            )

    def cross(u):
        k, c0, width, _ = units[u]
        rows = rows_at(4 * OWNED * (1 - side), 4 * OWNED)
        cols = pl.ds(c0, width)
        crossed[u] = start(c_send.at[k, rows, cols], c_cross.at[k, :, cols], c_s.at[u, 6], c_r.at[u, 6], to_mate)

    def cross_done(u):
        k, c0, width, _ = units[u]
        cols = slice(c0, c0 + width)
        crossed[u].wait_recv()
        rows = rows_at(4 * OWNED * side, 4 * OWNED)
        total = corr[k, rows, cols] + c_cross[k, :, cols].astype(F32)
        corr[k, rows, cols] = total
        c_send[k, rows, cols] = total.astype(BF16)
        send_along_x(u)

    weights, passed = {}, {}

    def send_weights(u, slot, rows, peer):
        k, c0, width, _ = units[u]
        part = w_buf.at[k, rows, pl.ds(c0, width)]
        return start(part, part, w_s.at[u, slot], w_r.at[u, slot], peer)

    def sum_along_x(u):
        k, c0, width, order = units[u]
        cols = slice(c0, c0 + width)
        base, count = layout(order)
        for handle in near[u]:
            handle.wait_recv()
        rows = rows_at(base(across), count)
        return (
            corr[k, rows, cols] + c_right[k, 0:count, cols].astype(F32) + c_left[k, 0:count, cols].astype(F32)
        )

    def store_weights(u, total):
        k, c0, width, order = units[u]
        w_buf[k, own_rows(order, side), c0 : c0 + width] = (total * scale_off).astype(BF16)

    def reduce_x(u):
        k, c0, width, order = units[u]
        cols = slice(c0, c0 + width)
        corr[k, rows_at(2 * OWNED * across, 2 * OWNED), cols] = sum_along_x(u)
        theirs = own_rows(order, 1 - side)
        c_send[k, theirs, cols] = corr[k, theirs, cols].astype(BF16)
        crossed[u] = start(
            c_send.at[k, theirs, pl.ds(c0, width)], c_cross.at[k, pl.ds(0, OWNED), pl.ds(c0, width)],
            c_s.at[u, 6], c_r.at[u, 6], to_mate,
        )

    def reduce_done(u):
        k, c0, width, order = units[u]
        cols = slice(c0, c0 + width)
        mine = own_rows(order, side)
        if order == "x":
            crossed[u].wait_recv()
            store_weights(u, corr[k, mine, cols] + c_cross[k, 0:OWNED, cols].astype(F32))
            weights[u] = [send_weights(u, 6, mine, to_mate)]
        else:
            store_weights(u, sum_along_x(u))
            weights[u] = []
        passed[u] = [send_weights(u, 0, mine, to_right), send_weights(u, 1, mine, to_left)]

    def pass_mate(u):
        weights[u].pop().wait_recv()
        theirs = own_rows(units[u][3], 1 - side)
        passed[u] += [send_weights(u, 2, theirs, to_right), send_weights(u, 3, theirs, to_left)]

    def pass_far(u):
        base, count = layout(units[u][3])
        half = count // 2
        for handle in passed[u]:
            handle.wait_recv()
        weights[u] += [
            send_weights(u, 4, rows_at(base(left), half), to_right),
            send_weights(u, 5, rows_at(base(right) + half, half), to_left),
        ]
        if units[u][3] == "y":
            passed[u] = [
                send_weights(u, 6 + n, rows_at(base(x), OWNED), to_mate) for n, x in enumerate((across, right, left))
            ]
        else:
            passed[u] = []

    def pass_last(u):
        for handle in weights[u]:
            handle.wait_recv()
        base, _ = layout("y")
        passed[u].append(send_weights(u, 9, rows_at(base(opposite), OWNED), to_mate))

    def gathered(u):
        for handle in passed[u] if units[u][3] == "y" else weights[u]:
            handle.wait_recv()

    rescale_a(0)
    rescale_b(0)
    correlate(0, 0)
    half_a = half_of(va, center_a, inverse_a)
    half_b = half_of(vb, center_b, inverse_b)
    shared_a = a_buf[0, 0:ROWS].astype(F32)
    shared_b = b_buf[0, 0:ROWS].astype(F32)
    mid[0] = jnp.concatenate(
        [column_sum(t) for t in (half_a * half_b, shared_a, shared_b, half_a, half_b)] + [zero_row] * 3, axis=0
    )
    mid_arrive = [start(mid.at[0], mid.at[r], mid_s.at[r], mid_r.at[r], dp_peer[r]) for r in range(1, 8)]
    a_near[1].wait_recv()
    rescale_a(1)
    correlate(0, 1)
    send_along_x(0)
    a_near[2].wait_recv()
    a_far = start(a_raw.at[2], a_raw.at[3], a_s.at[3], a_r.at[3], j_peer[1])
    b_far = []
    for r, first in ((1, 0), (3, ROWS // 2)):
        b_near[r].wait_recv()
        half = pl.ds(first, ROWS // 2)
        n = 2 if r == 1 else 0
        b_far.append(start(b_raw.at[r, half], b_raw.at[2, half], b_s.at[n], b_r.at[n], z_peer[4 - r]))
    relay(0)
    rescale_a(2)
    rescale_b(1)
    rescale_b(3)
    for k in (1, 3):
        for m in range(3):
            correlate(k, m)
    a_far.wait_recv()
    rescale_a(3)
    correlate(3, 3)
    cross(2)
    correlate(1, 3)
    send_along_x(1)
    correlate(0, 2)
    correlate(0, 3)
    cross(4)
    for handle in mid_arrive:
        handle.wait_recv()
    totals = tree_sum([mid[r] for r in range(8)])
    sums_a[0] = totals
    sums_b[0] = totals
    sum_arrive = [start(sums_a.at[0], sums_a.at[r], sum_s.at[r], sum_r.at[r], j_peer[r]) for r in range(1, 4)]
    sum_arrive += [start(sums_b.at[0], sums_b.at[r], sum_s.at[3 + r], sum_r.at[3 + r], z_peer[r]) for r in range(1, 4)]
    diagonal = totals[0:1] / BATCH
    diag_weight = (-2.0 * (1.0 - diagonal)).astype(BF16).astype(F32)
    cross_done(2)
    relay(1)
    for handle in b_far:
        handle.wait_recv()
    rescale_b(2)
    for m in range(4):
        correlate(2, m)
    send_along_x(3)
    cross_done(4)
    relay(2)
    reduce_x(1)
    relay(3)
    reduce_done(1)
    reduce_x(0)
    relay(4)
    reduce_done(2)
    pass_mate(1)
    reduce_x(3)
    pass_far(2)
    reduce_done(4)
    reduce_done(0)
    pass_far(1)
    reduce_done(3)
    pass_last(2)
    pass_far(4)
    for handle in sum_arrive:
        handle.wait_recv()
    for r in range(4):
        for sums_ref, row, buf in ((sums_a, 1, a_buf), (sums_b, 2, b_buf)):
            value = sums_ref[r, row : row + 1]
            high = value.astype(BF16)
            low = (value - high.astype(F32)).astype(BF16)
            buf[r, ROWS : ROWS + EXTRA] = jnp.concatenate(
                [high.astype(F32), low.astype(F32), jnp.zeros((EXTRA - 2, COLS), F32)], axis=0
            ).astype(BF16)
    pass_mate(3)
    pass_mate(0)

    ub_arrive = {}
    vecb_arrive = {}
    ua_done = set()

    def squares(k):
        square = jnp.square(w_buf[k].astype(F32))
        if ua_done:
            second_acc[0:1] += column_sum(square)
        else:
            second_acc[0:1] = column_sum(square)
        folded = sum(square[:, i * 128 : (i + 1) * 128] for i in range(8))
        return column_sum(folded.T)

    def upstream_of_b(k, over_first):
        total = None
        for m in range(4):
            term = matmul(a_buf[m], w_buf[k, :, m * COLS : (m + 1) * COLS], ((1,), (1,)))
            total = term if total is None else total + term
        if k == 0:
            ub_own[...] = total[0:ROWS]
        else:
            ub_send[k] = (total[0:ROWS] - b_buf[k, 0:ROWS].astype(F32) * (over_first * along)).astype(BF16)
            ub_arrive[k] = start(ub_send.at[k], ub_recv.at[k], ub_s.at[k], ub_r.at[k], z_peer[k])
        first = total[ROWS : ROWS + 1] + total[ROWS + 1 : ROWS + 2]
        slot = vec_b.at[0 if k == 0 else 3 + k]
        slot[...] = jnp.concatenate([first, over_first] + [zero_row] * 6, axis=0)
        if k:
            vecb_arrive[k] = start(slot, vec_b.at[k], vec_s.at[3 + k], vec_r.at[3 + k], z_peer[k])

    def upstream_of_a(k, m):
        term = matmul(b_buf[k], w_buf[k, :, m * COLS : (m + 1) * COLS], ((1,), (0,)))
        if m in ua_done:
            ua_acc[m] += term
        else:
            ua_acc[m] = term
            ua_done.add(m)

    def take_out(r):
        taken = second_acc[0:1, r * COLS : (r + 1) * COLS] * along
        ua_acc[r, 0:ROWS] -= a_buf[r, 0:ROWS].astype(F32) * taken

    gathered(1)
    over_first = squares(1)
    upstream_of_b(1, over_first)
    for m in range(4):
        upstream_of_a(1, m)
    pass_far(3)
    pass_far(0)
    pass_last(4)
    gathered(2)
    over_first = squares(3)
    upstream_of_b(3, over_first)
    for m in range(4):
        upstream_of_a(3, m)
    gathered(3)
    over_first = squares(2)
    upstream_of_b(2, over_first)
    for m in range(4):
        upstream_of_a(2, m)
    gathered(0)
    gathered(4)
    over_first = squares(0)
    upstream_of_a(0, 3)
    take_out(3)
    ua3 = start(ua_acc.at[3, pl.ds(0, ROWS)], ua_near.at[1], ua_s.at[3], ua_r.at[3], j_peer[1])
    upstream_of_a(0, 2)
    take_out(2)
    ua3.wait_recv()
    ua_send[...] = (ua_acc[2, 0:ROWS] + ua_near[1]).astype(BF16)
    ua2 = start(ua_send, ua_recv, ua_s.at[2], ua_r.at[2], j_peer[2])
    upstream_of_a(0, 1)
    ua1 = start(ua_acc.at[1, pl.ds(0, ROWS)], ua_near.at[0], ua_s.at[1], ua_r.at[1], j_peer[1])
    upstream_of_a(0, 0)
    upstream_of_b(0, over_first)

    block_sum = sum(second_acc[0:1, m * COLS : (m + 1) * COLS] for m in range(4))
    loss_row = (1.0 - diagonal) ** 2 + (0.25 / off_weight) * block_sum
    vec_arrive = []
    for r in range(4):
        first = ua_acc[r, ROWS : ROWS + 1] + ua_acc[r, ROWS + 1 : ROWS + 2]
        second = second_acc[0:1, r * COLS : (r + 1) * COLS]
        slot = vec_a.at[0 if r == 0 else 3 + r]
        slot[...] = jnp.concatenate([first, second, loss_row] + [zero_row] * 5, axis=0)
        if r:
            vec_arrive.append(start(slot, vec_a.at[r], vec_s.at[r], vec_r.at[r], j_peer[r]))
    for handle in vec_arrive:
        handle.wait_recv()
    sum_a = tree_sum([vec_a[r] for r in range(4)])
    vec_l[0] = sum_a
    loss_arrive = [start(vec_l.at[0], vec_l.at[r], vl_s.at[r], vl_r.at[r], z_peer[r]) for r in range(1, 4)]
    for handle in vecb_arrive.values():
        handle.wait_recv()
    sum_b = tree_sum([vec_b[r] for r in range(4)])
    for handle in loss_arrive:
        handle.wait_recv()
    losses = tree_sum([vec_l[r] for r in range(4)])
    loss[...] = jnp.sum(losses[2:3], axis=1, keepdims=True) / D

    def finish(upstream, view, center, inverse, own_sum, sums, out):
        first = (sums[0:1] + diag_weight * own_sum) / BATCH
        second = sums[1:2] * along + diag_weight * diagonal
        normed = (view[...] - center) * inverse
        out[...] = (upstream - first - normed * second) * inverse

    for k in (1, 3, 2):
        ub_arrive[k].wait_recv()
    upstream_b = ub_own[...] + sum(ub_recv[k].astype(F32) for k in (1, 2, 3)) + diag_weight * half_of(va, center_a, inverse_a)
    taken = (vec_b[1, 1:2] + vec_b[2, 1:2] + vec_b[3, 1:2]) * along
    upstream_b = upstream_b + taken * b_buf[0, 0:ROWS].astype(F32)
    finish(upstream_b, vb, center_b, inverse_b, totals[3:4], sum_b, gb)
    ua1.wait_recv()
    taken = (vec_a[2, 1:2] + vec_a[3, 1:2]) * along
    upstream_a = ua_acc[0, 0:ROWS] + ua_near[0] + diag_weight * half_of(vb, center_b, inverse_b)
    upstream_a = upstream_a + taken * a_buf[0, 0:ROWS].astype(F32)
    finish(upstream_a, va, center_a, inverse_a, totals[4:5], sum_a, ga)
    for handle in pending:
        if handle is not ua2:
            handle.wait_send()
    ua2.wait_recv()
    ga[...] += ua_recv[...].astype(F32) * inverse_a
    ua2.wait_send()


def per_device(view_a, view_b):
    view = VMEM((ROWS, COLS), F32)
    small = VMEM((8, 8, COLS), F32)
    block = VMEM((4, ROWS + EXTRA, COLS), BF16)
    plain = VMEM((4, ROWS, COLS), BF16)
    chunk = (4, COLS, WIDE)
    pair = VMEM((4, 2 * OWNED, WIDE), BF16)
    grad_a, grad_b, loss = pl.pallas_call(
        kernel,
        out_shape=(
            jax.ShapeDtypeStruct((ROWS, COLS), F32),
            jax.ShapeDtypeStruct((ROWS, COLS), F32),
            jax.ShapeDtypeStruct((1, 1), F32),
        ),
        in_specs=[pl.BlockSpec(memory_space=pltpu.HBM)] * 2,
        out_specs=[pl.BlockSpec(memory_space=VMEM)] * 3,
        scratch_shapes=[
            view, view, small, small, small, small, small, small, small,
            VMEM((4, 8, COLS), F32), VMEM((4, 8, COLS), F32), plain, plain, block, block, VMEM((4, COLS, ROWS), BF16), VMEM(chunk, F32), VMEM(chunk, BF16), pair, pair, pair, VMEM((4, 4 * OWNED, WIDE), BF16),
            VMEM(chunk, BF16),
            VMEM((4, ROWS + EXTRA, COLS), F32), VMEM((ROWS, COLS), F32),
            VMEM((2, ROWS, COLS), F32), VMEM((ROWS, COLS), BF16), VMEM((ROWS, COLS), BF16), plain, plain, VMEM((8, WIDE), F32),
            DMA((2,)), *[DMA((8,))] * 12, *[DMA((4,))] * 4, *[DMA((5, 10))] * 4, *[DMA((4,))] * 4,
        ],
        compiler_params=pltpu.CompilerParams(
            collective_id=0, has_side_effects=True, vmem_limit_bytes=44 * 1024 * 1024
        ),
        cost_estimate=pl.CostEstimate(flops=3 * 2 * 1024**3, bytes_accessed=4 * 1024 * 1024, transcendentals=0),
        name="twins",
    )(view_a, view_b)
    return grad_a, grad_b, loss[0, 0]


def solution(mesh):
    in_specs = (P("dp", "feat"), P("dp", "feat"))
    out_specs = (P("dp", "feat"), P("dp", "feat"), P())
    return jax.shard_map(
        per_device, mesh=mesh, in_specs=in_specs, out_specs=out_specs, check_vma=False
    )
```

```python
import functools

import jax
import jax.numpy as jnp
from jax import lax
from jax.experimental import pallas as pl
from jax.experimental.pallas import tpu as pltpu
from jax.sharding import PartitionSpec as P

D = 4096
BATCH = 8192
ROWS = 1024
COLS = 256
WIDE = 4 * COLS
EXTRA = 16
OWNED = COLS // 8

off_weight = 0.0051
variance_eps = 1e-05
scale_off = 2.0 * off_weight / BATCH
along = 0.5 / off_weight

MESH = pl.DeviceIdType.MESH
BF16 = jnp.bfloat16
F32 = jnp.float32
VMEM = pltpu.VMEM
DMA = pltpu.SemaphoreType.DMA


def flip(index, mask):
    for bit in (1, 2, 4, 8):
        if mask & bit:
            index = index + bit - 2 * bit * ((index // bit) % 2)
    return index


def tree_sum(terms):
    while len(terms) > 1:
        terms = [terms[i] + terms[i + 1] for i in range(0, len(terms), 2)]
    return terms[0]


def matmul(a, b, contract):
    return lax.dot_general(a, b, (contract, ((), ())), preferred_element_type=F32)


def column_sum(value):
    return jnp.sum(value, axis=0, keepdims=True)


def kernel(
    va_hbm, vb_hbm, ga, gb, loss,
    va, vb,
    stat, mid, sums_a, sums_b, vec_a, vec_b, vec_l,
    coef_j, coef_z, a_raw, b_raw, a_buf, b_buf, bt, corr, c_send, c_relay, c_right, c_left, c_cross, w_buf,
    ua_acc, ub_own, ua_near, ua_send, ua_recv, ub_send, ub_recv, second_acc,
    io, stat_s, stat_r, mid_s, mid_r, sum_s, sum_r, vec_s, vec_r, vl_s, vl_r,
    coef_s, coef_r, a_s, a_r, b_s, b_r, c_s, c_r, w_s, w_r, ua_s, ua_r, ub_s, ub_r,
):
    p = lax.axis_index("dp")
    f = lax.axis_index("feat")
    across = p // 2
    side = p % 2
    dp_peer = [(flip(p, r), f) for r in range(8)]
    j_peer = [(p, flip(f, r)) for r in range(4)]
    z_peer = [(p, flip(f, 4 * r)) for r in range(4)]
    pending = []

    def start(src, dst, send_sem, recv_sem, peer):
        handle = pltpu.make_async_remote_copy(
            src_ref=src, dst_ref=dst, send_sem=send_sem, recv_sem=recv_sem,
            device_id=peer, device_id_type=MESH,
        )
        handle.start()
        pending.append(handle)
        return handle

    barrier = pltpu.get_barrier_semaphore()
    for peer in dp_peer[1:] + j_peer[1:] + z_peer[1:]:
        pl.semaphore_signal(barrier, inc=1, device_id=peer, device_id_type=MESH)
    load_a = pltpu.make_async_copy(va_hbm, va, io.at[0])
    load_b = pltpu.make_async_copy(vb_hbm, vb, io.at[1])
    load_a.start()
    load_b.start()

    zero_row = jnp.zeros((1, COLS), F32)
    load_a.wait()
    mean_a = column_sum(va[...]) / ROWS
    square_a = column_sum((va[...] - mean_a) ** 2)
    load_b.wait()
    mean_b = column_sum(vb[...]) / ROWS
    square_b = column_sum((vb[...] - mean_b) ** 2)
    stat[0] = jnp.concatenate([mean_a, square_a, mean_b, square_b] + [zero_row] * 4, axis=0)
    local_a = jnp.sqrt(square_a / ROWS + variance_eps)
    local_b = jnp.sqrt(square_b / ROWS + variance_eps)
    whole = pl.ds(0, ROWS)
    a_raw[0] = ((va[...] - mean_a) * (1.0 / local_a)).astype(BF16)
    b_raw[0] = ((vb[...] - mean_b) * (1.0 / local_b)).astype(BF16)
    pl.semaphore_wait(barrier, 13)
    arrive = [start(stat.at[0], stat.at[r], stat_s.at[r], stat_r.at[r], dp_peer[r]) for r in range(1, 8)]
    b_near = {r: start(b_raw.at[0], b_raw.at[r], b_s.at[r], b_r.at[r], z_peer[r]) for r in (1, 3)}
    a_near = {r: start(a_raw.at[0], a_raw.at[r], a_s.at[r], a_r.at[r], j_peer[r]) for r in (1, 2)}
    for handle in arrive:
        handle.wait_recv()
    every = [stat[r] for r in range(8)]
    mean = tree_sum(every) / 8
    spreads = tree_sum([(t - mean) ** 2 for t in every]) * ROWS
    squares = tree_sum(every)
    center_a, center_b = mean[0:1], mean[2:3]
    spread_a = jnp.sqrt((squares[1:2] + spreads[0:1]) / BATCH + variance_eps)
    spread_b = jnp.sqrt((squares[3:4] + spreads[2:3]) / BATCH + variance_eps)
    inverse_a, inverse_b = 1.0 / spread_a, 1.0 / spread_b
    coef_j[0] = jnp.concatenate([local_a * inverse_a, (mean_a - center_a) * inverse_a] + [zero_row] * 6, axis=0)
    coef_z[0] = jnp.concatenate([local_b * inverse_b, (mean_b - center_b) * inverse_b] + [zero_row] * 6, axis=0)
    coef_arrive = {}
    for n, (coef, peers) in enumerate(((coef_j, j_peer), (coef_z, z_peer))):
        for r in range(1, 4):
            coef_arrive[n, r] = start(coef.at[0], coef.at[r], coef_s.at[4 * n + r], coef_r.at[4 * n + r], peers[r])

    def half_of(view, center, inverse):
        return ((view[...] - center) * inverse).astype(BF16).astype(F32)

    def rescale_a(r):
        if r:
            coef_arrive[0, r].wait_recv()
        a_buf[r, 0:ROWS] = (a_raw[r].astype(F32) * coef_j[r, 0:1] + coef_j[r, 1:2]).astype(BF16)

    def rescale_b(r):
        if r:
            coef_arrive[1, r].wait_recv()
        b_buf[r, 0:ROWS] = (b_raw[r].astype(F32) * coef_z[r, 0:1] + coef_z[r, 1:2]).astype(BF16)
        bt[r] = b_buf[r, 0:ROWS].T

    def correlate(k, m):
        block = matmul(bt[k], a_buf[m, 0:ROWS], ((1,), (0,)))
        if k == 0 and m == 0:
            same = lax.broadcasted_iota(jnp.int32, block.shape, 0) == lax.broadcasted_iota(jnp.int32, block.shape, 1)
            block = jnp.where(same, 0.0, block)
        corr[k, :, m * COLS : (m + 1) * COLS] = block
        c_send[k, :, m * COLS : (m + 1) * COLS] = block.astype(BF16)

    units = [
        (0, 0, WIDE // 2, "x"), (1, 0, WIDE, "x"), (3, 0, WIDE, "y"), (2, 0, WIDE, "x"), (0, WIDE // 2, WIDE // 2, "y"),
    ]
    right, opposite, left = (flip(across, r) for r in (1, 2, 3))
    to_right, to_left, to_mate = dp_peer[2], dp_peer[6], dp_peer[1]

    def rows_at(first, count):
        return pl.ds(pl.multiple_of(first, 16), count)

    def layout(order):
        if order == "x":
            return (lambda x: 2 * OWNED * x), 2 * OWNED
        return (lambda x: 4 * OWNED * side + OWNED * x), OWNED

    def own_rows(order, whose):
        first = 2 * OWNED * across + OWNED * whose if order == "x" else 4 * OWNED * whose + OWNED * across
        return rows_at(first, OWNED)

    near, relays, crossed = {}, {}, {}

    def send_sum(u, first, count, dst, slot, peer):
        k, c0, width, _ = units[u]
        cols = pl.ds(c0, width)
        return start(c_send.at[k, rows_at(first, count), cols], dst.at[k, :, cols], c_s.at[u, slot], c_r.at[u, slot], peer)

    def send_along_x(u):
        base, count = layout(units[u][3])
        half = count // 2
        k, c0, width, _ = units[u]
        cols = pl.ds(c0, width)

        def part(x, which, dst, slot, peer):
            return start(
                c_send.at[k, rows_at(base(x) + which * half, half), cols],
                dst.at[k, pl.ds(which * half, half), cols], c_s.at[u, slot], c_r.at[u, slot], peer,
            )

        relays[u] = [part(opposite, 0, c_relay, 0, to_right), part(opposite, 1, c_relay, 1, to_left)]
        near[u] = [part(right, 0, c_right, 2, to_right), part(left, 1, c_left, 3, to_left)]

    def relay(u):
        k, c0, width, order = units[u]
        base, count = layout(order)
        half = count // 2
        cols = slice(c0, c0 + width)
        ends = ((0, left, c_left, 4, to_left), (1, right, c_right, 5, to_right))
        for which, x, dst, slot, peer in ends:
            relays[u][which].wait_recv()
            rows = rows_at(base(x) + which * half, half)
            got = c_relay[k, which * half : (which + 1) * half, cols].astype(F32)
            c_send[k, rows, cols] = (corr[k, rows, cols] + got).astype(BF16)
            near[u].append(
                start(
                    c_send.at[k, rows, pl.ds(c0, width)], dst.at[k, pl.ds(which * half, half), pl.ds(c0, width)],
                    c_s.at[u, slot], c_r.at[u, slot], peer,
                )
            )

    def cross(u):
        k, c0, width, _ = units[u]
        rows = rows_at(4 * OWNED * (1 - side), 4 * OWNED)
        cols = pl.ds(c0, width)
        crossed[u] = start(c_send.at[k, rows, cols], c_cross.at[k, :, cols], c_s.at[u, 6], c_r.at[u, 6], to_mate)

    def cross_done(u):
        k, c0, width, _ = units[u]
        cols = slice(c0, c0 + width)
        crossed[u].wait_recv()
        rows = rows_at(4 * OWNED * side, 4 * OWNED)
        total = corr[k, rows, cols] + c_cross[k, :, cols].astype(F32)
        corr[k, rows, cols] = total
        c_send[k, rows, cols] = total.astype(BF16)
        send_along_x(u)

    weights, passed = {}, {}

    def send_weights(u, slot, rows, peer):
        k, c0, width, _ = units[u]
        part = w_buf.at[k, rows, pl.ds(c0, width)]
        return start(part, part, w_s.at[u, slot], w_r.at[u, slot], peer)

    def sum_along_x(u):
        k, c0, width, order = units[u]
        cols = slice(c0, c0 + width)
        base, count = layout(order)
        for handle in near[u]:
            handle.wait_recv()
        rows = rows_at(base(across), count)
        return (
            corr[k, rows, cols] + c_right[k, 0:count, cols].astype(F32) + c_left[k, 0:count, cols].astype(F32)
        )

    def store_weights(u, total):
        k, c0, width, order = units[u]
        w_buf[k, own_rows(order, side), c0 : c0 + width] = (total * scale_off).astype(BF16)

    def reduce_x(u):
        k, c0, width, order = units[u]
        cols = slice(c0, c0 + width)
        corr[k, rows_at(2 * OWNED * across, 2 * OWNED), cols] = sum_along_x(u)
        theirs = own_rows(order, 1 - side)
        c_send[k, theirs, cols] = corr[k, theirs, cols].astype(BF16)
        crossed[u] = start(
            c_send.at[k, theirs, pl.ds(c0, width)], c_cross.at[k, pl.ds(0, OWNED), pl.ds(c0, width)],
            c_s.at[u, 6], c_r.at[u, 6], to_mate,
        )

    def reduce_done(u):
        k, c0, width, order = units[u]
        cols = slice(c0, c0 + width)
        mine = own_rows(order, side)
        if order == "x":
            crossed[u].wait_recv()
            store_weights(u, corr[k, mine, cols] + c_cross[k, 0:OWNED, cols].astype(F32))
            weights[u] = [send_weights(u, 6, mine, to_mate)]
        else:
            store_weights(u, sum_along_x(u))
            weights[u] = []
        passed[u] = [send_weights(u, 0, mine, to_right), send_weights(u, 1, mine, to_left)]

    def pass_mate(u):
        weights[u].pop().wait_recv()
        theirs = own_rows(units[u][3], 1 - side)
        passed[u] += [send_weights(u, 2, theirs, to_right), send_weights(u, 3, theirs, to_left)]

    def pass_far(u):
        base, count = layout(units[u][3])
        half = count // 2
        for handle in passed[u]:
            handle.wait_recv()
        weights[u] += [
            send_weights(u, 4, rows_at(base(left), half), to_right),
            send_weights(u, 5, rows_at(base(right) + half, half), to_left),
        ]
        if units[u][3] == "y":
            passed[u] = [
                send_weights(u, 6 + n, rows_at(base(x), OWNED), to_mate) for n, x in enumerate((across, right, left))
            ]
        else:
            passed[u] = []

    def pass_last(u):
        for handle in weights[u]:
            handle.wait_recv()
        base, _ = layout("y")
        passed[u].append(send_weights(u, 9, rows_at(base(opposite), OWNED), to_mate))

    def gathered(u):
        for handle in passed[u] if units[u][3] == "y" else weights[u]:
            handle.wait_recv()

    rescale_a(0)
    rescale_b(0)
    correlate(0, 0)
    a_near[1].wait_recv()
    rescale_a(1)
    correlate(0, 1)
    send_along_x(0)
    a_near[2].wait_recv()
    a_far = start(a_raw.at[2], a_raw.at[3], a_s.at[3], a_r.at[3], j_peer[1])
    b_far = []
    for r, first in ((1, 0), (3, ROWS // 2)):
        b_near[r].wait_recv()
        half = pl.ds(first, ROWS // 2)
        n = 2 if r == 1 else 0
        b_far.append(start(b_raw.at[r, half], b_raw.at[2, half], b_s.at[n], b_r.at[n], z_peer[4 - r]))
    relay(0)
    rescale_a(2)
    rescale_b(1)
    rescale_b(3)
    for k in (1, 3):
        for m in range(3):
            correlate(k, m)
    a_far.wait_recv()
    rescale_a(3)
    correlate(3, 3)
    cross(2)
    correlate(1, 3)
    send_along_x(1)
    correlate(0, 2)
    correlate(0, 3)
    cross(4)
    half_a = half_of(va, center_a, inverse_a)
    half_b = half_of(vb, center_b, inverse_b)
    shared_a = a_buf[0, 0:ROWS].astype(F32)
    shared_b = b_buf[0, 0:ROWS].astype(F32)
    mid[0] = jnp.concatenate(
        [column_sum(t) for t in (half_a * half_b, shared_a, shared_b, half_a, half_b)] + [zero_row] * 3, axis=0
    )
    mid_arrive = [start(mid.at[0], mid.at[r], mid_s.at[r], mid_r.at[r], dp_peer[r]) for r in range(1, 8)]
    cross_done(2)
    relay(1)
    for handle in b_far:
        handle.wait_recv()
    rescale_b(2)
    for m in range(4):
        correlate(2, m)
    send_along_x(3)
    cross_done(4)
    relay(2)
    reduce_x(1)
    for handle in mid_arrive:
        handle.wait_recv()
    totals = tree_sum([mid[r] for r in range(8)])
    sums_a[0] = totals
    sums_b[0] = totals
    sum_arrive = [start(sums_a.at[0], sums_a.at[r], sum_s.at[r], sum_r.at[r], j_peer[r]) for r in range(1, 4)]
    sum_arrive += [start(sums_b.at[0], sums_b.at[r], sum_s.at[3 + r], sum_r.at[3 + r], z_peer[r]) for r in range(1, 4)]
    diagonal = totals[0:1] / BATCH
    diag_weight = (-2.0 * (1.0 - diagonal)).astype(BF16).astype(F32)
    relay(3)
    reduce_done(1)
    reduce_x(0)
    relay(4)
    reduce_done(2)
    pass_mate(1)
    reduce_x(3)
    pass_far(2)
    reduce_done(4)
    reduce_done(0)
    pass_far(1)
    reduce_done(3)
    pass_last(2)
    pass_far(4)
    for handle in sum_arrive:
        handle.wait_recv()
    for r in range(4):
        for sums_ref, row, buf in ((sums_a, 1, a_buf), (sums_b, 2, b_buf)):
            value = sums_ref[r, row : row + 1]
            high = value.astype(BF16)
            low = (value - high.astype(F32)).astype(BF16)
            buf[r, ROWS : ROWS + EXTRA] = jnp.concatenate(
                [high.astype(F32), low.astype(F32), jnp.zeros((EXTRA - 2, COLS), F32)], axis=0
            ).astype(BF16)
    pass_mate(3)
    pass_mate(0)

    ub_arrive = {}
    vecb_arrive = {}
    ua_done = set()

    def squares(k):
        square = jnp.square(w_buf[k].astype(F32))
        if ua_done:
            second_acc[0:1] += column_sum(square)
        else:
            second_acc[0:1] = column_sum(square)
        folded = sum(square[:, i * 128 : (i + 1) * 128] for i in range(8))
        return column_sum(folded.T)

    def upstream_of_b(k, over_first):
        total = None
        for m in range(4):
            term = matmul(a_buf[m], w_buf[k, :, m * COLS : (m + 1) * COLS], ((1,), (1,)))
            total = term if total is None else total + term
        first = total[ROWS : ROWS + 1] + total[ROWS + 1 : ROWS + 2]
        slot = vec_b.at[0 if k == 0 else 3 + k]
        slot[...] = jnp.concatenate([first, over_first] + [zero_row] * 6, axis=0)
        if k:
            vecb_arrive[k] = start(slot, vec_b.at[k], vec_s.at[3 + k], vec_r.at[3 + k], z_peer[k])
        if k == 0:
            ub_own[...] = total[0:ROWS]
        else:
            ub_send[k] = (total[0:ROWS] - b_buf[k, 0:ROWS].astype(F32) * (over_first * along)).astype(BF16)
            ub_arrive[k] = start(ub_send.at[k], ub_recv.at[k], ub_s.at[k], ub_r.at[k], z_peer[k])

    def upstream_of_a(k, m):
        term = matmul(b_buf[k], w_buf[k, :, m * COLS : (m + 1) * COLS], ((1,), (0,)))
        if m in ua_done:
            ua_acc[m] += term
        else:
            ua_acc[m] = term
            ua_done.add(m)

    def take_out(r):
        taken = second_acc[0:1, r * COLS : (r + 1) * COLS] * along
        ua_acc[r, 0:ROWS] -= a_buf[r, 0:ROWS].astype(F32) * taken

    gathered(1)
    over_first = squares(1)
    upstream_of_b(1, over_first)
    for m in range(4):
        upstream_of_a(1, m)
    pass_far(3)
    pass_far(0)
    pass_last(4)
    gathered(2)
    over_first = squares(3)
    upstream_of_b(3, over_first)
    for m in range(4):
        upstream_of_a(3, m)
    gathered(3)
    over_first = squares(2)
    upstream_of_b(2, over_first)
    for m in range(4):
        upstream_of_a(2, m)
    gathered(0)
    gathered(4)
    over_first = squares(0)
    for m in (3, 1, 2, 0):
        upstream_of_a(0, m)
        if m == 3:
            take_out(3)
            ua3 = start(ua_acc.at[3, pl.ds(0, ROWS)], ua_near.at[1], ua_s.at[3], ua_r.at[3], j_peer[1])
    ua1 = start(ua_acc.at[1, pl.ds(0, ROWS)], ua_near.at[0], ua_s.at[1], ua_r.at[1], j_peer[1])
    take_out(2)

    block_sum = sum(second_acc[0:1, m * COLS : (m + 1) * COLS] for m in range(4))
    loss_row = (1.0 - diagonal) ** 2 + (0.25 / off_weight) * block_sum
    vec_arrive = []
    for r in range(4):
        first = ua_acc[r, ROWS : ROWS + 1] + ua_acc[r, ROWS + 1 : ROWS + 2]
        second = second_acc[0:1, r * COLS : (r + 1) * COLS]
        slot = vec_a.at[0 if r == 0 else 3 + r]
        slot[...] = jnp.concatenate([first, second, loss_row] + [zero_row] * 5, axis=0)
        if r:
            vec_arrive.append(start(slot, vec_a.at[r], vec_s.at[r], vec_r.at[r], j_peer[r]))
    ua3.wait_recv()
    ua_send[...] = (ua_acc[2, 0:ROWS] + ua_near[1]).astype(BF16)
    ua2 = start(ua_send, ua_recv, ua_s.at[2], ua_r.at[2], j_peer[2])
    upstream_of_b(0, over_first)
    for handle in vec_arrive:
        handle.wait_recv()
    sum_a = tree_sum([vec_a[r] for r in range(4)])
    vec_l[0] = sum_a
    loss_arrive = [start(vec_l.at[0], vec_l.at[r], vl_s.at[r], vl_r.at[r], z_peer[r]) for r in range(1, 4)]
    for handle in vecb_arrive.values():
        handle.wait_recv()
    sum_b = tree_sum([vec_b[r] for r in range(4)])
    def finish(upstream, view, center, inverse, own_sum, sums, out):
        first = (sums[0:1] + diag_weight * own_sum) / BATCH
        second = sums[1:2] * along + diag_weight * diagonal
        normed = (view[...] - center) * inverse
        out[...] = (upstream - first - normed * second) * inverse

    for k in (1, 3, 2):
        ub_arrive[k].wait_recv()
    upstream_b = ub_own[...] + sum(ub_recv[k].astype(F32) for k in (1, 2, 3)) + diag_weight * half_of(va, center_a, inverse_a)
    taken = (vec_b[1, 1:2] + vec_b[2, 1:2] + vec_b[3, 1:2]) * along
    upstream_b = upstream_b + taken * b_buf[0, 0:ROWS].astype(F32)
    finish(upstream_b, vb, center_b, inverse_b, totals[3:4], sum_b, gb)
    ua1.wait_recv()
    taken = (vec_a[2, 1:2] + vec_a[3, 1:2]) * along
    upstream_a = ua_acc[0, 0:ROWS] + ua_near[0] + diag_weight * half_of(vb, center_b, inverse_b)
    upstream_a = upstream_a + taken * a_buf[0, 0:ROWS].astype(F32)
    finish(upstream_a, va, center_a, inverse_a, totals[4:5], sum_a, ga)
    for handle in loss_arrive:
        handle.wait_recv()
    losses = tree_sum([vec_l[r] for r in range(4)])
    loss[...] = jnp.sum(losses[2:3], axis=1, keepdims=True) / D
    for handle in pending:
        if handle is not ua2:
            handle.wait_send()
    ua2.wait_recv()
    ga[...] += ua_recv[...].astype(F32) * inverse_a
    ua2.wait_send()


def per_device(view_a, view_b):
    view = VMEM((ROWS, COLS), F32)
    small = VMEM((8, 8, COLS), F32)
    block = VMEM((4, ROWS + EXTRA, COLS), BF16)
    plain = VMEM((4, ROWS, COLS), BF16)
    chunk = (4, COLS, WIDE)
    pair = VMEM((4, 2 * OWNED, WIDE), BF16)
    grad_a, grad_b, loss = pl.pallas_call(
        kernel,
        out_shape=(
            jax.ShapeDtypeStruct((ROWS, COLS), F32),
            jax.ShapeDtypeStruct((ROWS, COLS), F32),
            jax.ShapeDtypeStruct((1, 1), F32),
        ),
        in_specs=[pl.BlockSpec(memory_space=pltpu.HBM)] * 2,
        out_specs=[pl.BlockSpec(memory_space=VMEM)] * 3,
        scratch_shapes=[
            view, view, small, small, small, small, small, small, small,
            VMEM((4, 8, COLS), F32), VMEM((4, 8, COLS), F32), plain, plain, block, block, VMEM((4, COLS, ROWS), BF16), VMEM(chunk, F32), VMEM(chunk, BF16), pair, pair, pair, VMEM((4, 4 * OWNED, WIDE), BF16),
            VMEM(chunk, BF16),
            VMEM((4, ROWS + EXTRA, COLS), F32), VMEM((ROWS, COLS), F32),
            VMEM((2, ROWS, COLS), F32), VMEM((ROWS, COLS), BF16), VMEM((ROWS, COLS), BF16), plain, plain, VMEM((8, WIDE), F32),
            DMA((2,)), *[DMA((8,))] * 12, *[DMA((4,))] * 4, *[DMA((5, 10))] * 4, *[DMA((4,))] * 4,
        ],
        compiler_params=pltpu.CompilerParams(
            collective_id=0, has_side_effects=True, vmem_limit_bytes=44 * 1024 * 1024
        ),
        cost_estimate=pl.CostEstimate(flops=3 * 2 * 1024**3, bytes_accessed=4 * 1024 * 1024, transcendentals=0),
        name="twins",
    )(view_a, view_b)
    return grad_a, grad_b, loss[0, 0]


def solution(mesh):
    in_specs = (P("dp", "feat"), P("dp", "feat"))
    out_specs = (P("dp", "feat"), P("dp", "feat"), P())
    return jax.shard_map(
        per_device, mesh=mesh, in_specs=in_specs, out_specs=out_specs, check_vma=False
    )
```

```python
import functools

import jax
import jax.numpy as jnp
from jax import lax
from jax.experimental import pallas as pl
from jax.experimental.pallas import tpu as pltpu
from jax.sharding import PartitionSpec as P

D = 4096
BATCH = 8192
ROWS = 1024
COLS = 256
WIDE = 4 * COLS
EXTRA = 16
OWNED = COLS // 8

off_weight = 0.0051
variance_eps = 1e-05
scale_off = 2.0 * off_weight / BATCH
along = 0.5 / off_weight

MESH = pl.DeviceIdType.MESH
BF16 = jnp.bfloat16
F32 = jnp.float32
VMEM = pltpu.VMEM
DMA = pltpu.SemaphoreType.DMA


def flip(index, mask):
    for bit in (1, 2, 4, 8):
        if mask & bit:
            index = index + bit - 2 * bit * ((index // bit) % 2)
    return index


def tree_sum(terms):
    while len(terms) > 1:
        terms = [terms[i] + terms[i + 1] for i in range(0, len(terms), 2)]
    return terms[0]


def matmul(a, b, contract):
    return lax.dot_general(a, b, (contract, ((), ())), preferred_element_type=F32)


def column_sum(value):
    return jnp.sum(value, axis=0, keepdims=True)


def kernel(
    va_hbm, vb_hbm, ga, gb, loss,
    va, vb,
    stat, mid, sums_a, sums_b, vec_a, vec_b, vec_l,
    coef_j, coef_z, a_raw, b_raw, a_buf, b_buf, bt, corr, c_send, c_relay, c_right, c_left, c_cross, w_buf,
    ua_acc, ub_own, ua_near, ua_send, ua_recv, ub_send, ub_recv, second_acc,
    io, stat_s, stat_r, mid_s, mid_r, sum_s, sum_r, vec_s, vec_r, vl_s, vl_r,
    coef_s, coef_r, a_s, a_r, b_s, b_r, c_s, c_r, w_s, w_r, ua_s, ua_r, ub_s, ub_r,
):
    p = lax.axis_index("dp")
    f = lax.axis_index("feat")
    across = p // 2
    side = p % 2
    dp_peer = [(flip(p, r), f) for r in range(8)]
    j_peer = [(p, flip(f, r)) for r in range(4)]
    z_peer = [(p, flip(f, 4 * r)) for r in range(4)]
    pending = []

    def start(src, dst, send_sem, recv_sem, peer):
        handle = pltpu.make_async_remote_copy(
            src_ref=src, dst_ref=dst, send_sem=send_sem, recv_sem=recv_sem,
            device_id=peer, device_id_type=MESH,
        )
        handle.start()
        pending.append(handle)
        return handle

    barrier = pltpu.get_barrier_semaphore()
    for peer in dp_peer[1:] + j_peer[1:] + z_peer[1:]:
        pl.semaphore_signal(barrier, inc=1, device_id=peer, device_id_type=MESH)
    load_a = pltpu.make_async_copy(va_hbm, va, io.at[0])
    load_b = pltpu.make_async_copy(vb_hbm, vb, io.at[1])
    load_a.start()
    load_b.start()

    zero_row = jnp.zeros((1, COLS), F32)
    load_a.wait()
    mean_a = column_sum(va[...]) / ROWS
    square_a = column_sum((va[...] - mean_a) ** 2)
    load_b.wait()
    mean_b = column_sum(vb[...]) / ROWS
    square_b = column_sum((vb[...] - mean_b) ** 2)
    stat[0] = jnp.concatenate([mean_a, square_a, mean_b, square_b] + [zero_row] * 4, axis=0)
    local_a = jnp.sqrt(square_a / ROWS + variance_eps)
    local_b = jnp.sqrt(square_b / ROWS + variance_eps)
    whole = pl.ds(0, ROWS)
    a_raw[0] = ((va[...] - mean_a) * (1.0 / local_a)).astype(BF16)
    b_raw[0] = ((vb[...] - mean_b) * (1.0 / local_b)).astype(BF16)
    pl.semaphore_wait(barrier, 13)
    arrive = [start(stat.at[0], stat.at[r], stat_s.at[r], stat_r.at[r], dp_peer[r]) for r in range(1, 8)]
    b_near = {r: start(b_raw.at[0], b_raw.at[r], b_s.at[r], b_r.at[r], z_peer[r]) for r in (1, 3)}
    a_near = {r: start(a_raw.at[0], a_raw.at[r], a_s.at[r], a_r.at[r], j_peer[r]) for r in (1, 2)}
    for handle in arrive:
        handle.wait_recv()
    every = [stat[r] for r in range(8)]
    mean = tree_sum(every) / 8
    spreads = tree_sum([(t - mean) ** 2 for t in every]) * ROWS
    squares = tree_sum(every)
    center_a, center_b = mean[0:1], mean[2:3]
    spread_a = jnp.sqrt((squares[1:2] + spreads[0:1]) / BATCH + variance_eps)
    spread_b = jnp.sqrt((squares[3:4] + spreads[2:3]) / BATCH + variance_eps)
    inverse_a, inverse_b = 1.0 / spread_a, 1.0 / spread_b
    coef_j[0] = jnp.concatenate([local_a * inverse_a, (mean_a - center_a) * inverse_a] + [zero_row] * 6, axis=0)
    coef_z[0] = jnp.concatenate([local_b * inverse_b, (mean_b - center_b) * inverse_b] + [zero_row] * 6, axis=0)
    coef_arrive = {}
    for n, (coef, peers) in enumerate(((coef_j, j_peer), (coef_z, z_peer))):
        for r in range(1, 4):
            coef_arrive[n, r] = start(coef.at[0], coef.at[r], coef_s.at[4 * n + r], coef_r.at[4 * n + r], peers[r])

    def half_of(view, center, inverse):
        return ((view[...] - center) * inverse).astype(BF16).astype(F32)

    def rescale_a(r):
        if r:
            coef_arrive[0, r].wait_recv()
        a_buf[r, 0:ROWS] = (a_raw[r].astype(F32) * coef_j[r, 0:1] + coef_j[r, 1:2]).astype(BF16)

    def rescale_b(r):
        if r:
            coef_arrive[1, r].wait_recv()
        b_buf[r, 0:ROWS] = (b_raw[r].astype(F32) * coef_z[r, 0:1] + coef_z[r, 1:2]).astype(BF16)
        bt[r] = b_buf[r, 0:ROWS].T

    def correlate(k, m):
        block = matmul(bt[k], a_buf[m, 0:ROWS], ((1,), (0,)))
        if k == 0 and m == 0:
            same = lax.broadcasted_iota(jnp.int32, block.shape, 0) == lax.broadcasted_iota(jnp.int32, block.shape, 1)
            block = jnp.where(same, 0.0, block)
        corr[k, :, m * COLS : (m + 1) * COLS] = block
        c_send[k, :, m * COLS : (m + 1) * COLS] = block.astype(BF16)

    units = [
        (0, 0, WIDE // 2, "x"), (1, 0, WIDE, "x"), (3, 0, WIDE, "y"), (2, 0, WIDE, "x"), (0, WIDE // 2, WIDE // 2, "y"),
    ]
    right, opposite, left = (flip(across, r) for r in (1, 2, 3))
    to_right, to_left, to_mate = dp_peer[2], dp_peer[6], dp_peer[1]

    def rows_at(first, count):
        return pl.ds(pl.multiple_of(first, 16), count)

    def layout(order):
        if order == "x":
            return (lambda x: 2 * OWNED * x), 2 * OWNED
        return (lambda x: 4 * OWNED * side + OWNED * x), OWNED

    def own_rows(order, whose):
        first = 2 * OWNED * across + OWNED * whose if order == "x" else 4 * OWNED * whose + OWNED * across
        return rows_at(first, OWNED)

    near, relays, crossed = {}, {}, {}

    def send_sum(u, first, count, dst, slot, peer):
        k, c0, width, _ = units[u]
        cols = pl.ds(c0, width)
        return start(c_send.at[k, rows_at(first, count), cols], dst.at[k, :, cols], c_s.at[u, slot], c_r.at[u, slot], peer)

    def send_along_x(u):
        base, count = layout(units[u][3])
        half = count // 2
        k, c0, width, _ = units[u]
        cols = pl.ds(c0, width)

        def part(x, which, dst, slot, peer):
            return start(
                c_send.at[k, rows_at(base(x) + which * half, half), cols],
                dst.at[k, pl.ds(which * half, half), cols], c_s.at[u, slot], c_r.at[u, slot], peer,
            )

        relays[u] = [part(opposite, 0, c_relay, 0, to_right), part(opposite, 1, c_relay, 1, to_left)]
        near[u] = [part(right, 0, c_right, 2, to_right), part(left, 1, c_left, 3, to_left)]

    def relay(u):
        k, c0, width, order = units[u]
        base, count = layout(order)
        half = count // 2
        cols = slice(c0, c0 + width)
        ends = ((0, left, c_left, 4, to_left), (1, right, c_right, 5, to_right))
        for which, x, dst, slot, peer in ends:
            relays[u][which].wait_recv()
            rows = rows_at(base(x) + which * half, half)
            got = c_relay[k, which * half : (which + 1) * half, cols].astype(F32)
            c_send[k, rows, cols] = (corr[k, rows, cols] + got).astype(BF16)
            near[u].append(
                start(
                    c_send.at[k, rows, pl.ds(c0, width)], dst.at[k, pl.ds(which * half, half), pl.ds(c0, width)],
                    c_s.at[u, slot], c_r.at[u, slot], peer,
                )
            )

    def cross(u):
        k, c0, width, _ = units[u]
        rows = rows_at(4 * OWNED * (1 - side), 4 * OWNED)
        cols = pl.ds(c0, width)
        crossed[u] = start(c_send.at[k, rows, cols], c_cross.at[k, :, cols], c_s.at[u, 6], c_r.at[u, 6], to_mate)

    def cross_done(u):
        k, c0, width, _ = units[u]
        cols = slice(c0, c0 + width)
        crossed[u].wait_recv()
        rows = rows_at(4 * OWNED * side, 4 * OWNED)
        total = corr[k, rows, cols] + c_cross[k, :, cols].astype(F32)
        corr[k, rows, cols] = total
        c_send[k, rows, cols] = total.astype(BF16)
        send_along_x(u)

    weights, passed = {}, {}

    def send_weights(u, slot, rows, peer):
        k, c0, width, _ = units[u]
        part = w_buf.at[k, rows, pl.ds(c0, width)]
        return start(part, part, w_s.at[u, slot], w_r.at[u, slot], peer)

    def sum_along_x(u):
        k, c0, width, order = units[u]
        cols = slice(c0, c0 + width)
        base, count = layout(order)
        for handle in near[u]:
            handle.wait_recv()
        rows = rows_at(base(across), count)
        return (
            corr[k, rows, cols] + c_right[k, 0:count, cols].astype(F32) + c_left[k, 0:count, cols].astype(F32)
        )

    def store_weights(u, total):
        k, c0, width, order = units[u]
        w_buf[k, own_rows(order, side), c0 : c0 + width] = (total * scale_off).astype(BF16)

    def reduce_x(u):
        k, c0, width, order = units[u]
        cols = slice(c0, c0 + width)
        corr[k, rows_at(2 * OWNED * across, 2 * OWNED), cols] = sum_along_x(u)
        theirs = own_rows(order, 1 - side)
        c_send[k, theirs, cols] = corr[k, theirs, cols].astype(BF16)
        crossed[u] = start(
            c_send.at[k, theirs, pl.ds(c0, width)], c_cross.at[k, pl.ds(0, OWNED), pl.ds(c0, width)],
            c_s.at[u, 6], c_r.at[u, 6], to_mate,
        )

    def reduce_done(u):
        k, c0, width, order = units[u]
        cols = slice(c0, c0 + width)
        mine = own_rows(order, side)
        if order == "x":
            crossed[u].wait_recv()
            store_weights(u, corr[k, mine, cols] + c_cross[k, 0:OWNED, cols].astype(F32))
            weights[u] = [send_weights(u, 6, mine, to_mate)]
        else:
            store_weights(u, sum_along_x(u))
            weights[u] = []
        passed[u] = [send_weights(u, 0, mine, to_right), send_weights(u, 1, mine, to_left)]

    def pass_mate(u):
        weights[u].pop().wait_recv()
        theirs = own_rows(units[u][3], 1 - side)
        passed[u] += [send_weights(u, 2, theirs, to_right), send_weights(u, 3, theirs, to_left)]

    def pass_far(u):
        base, count = layout(units[u][3])
        half = count // 2
        for handle in passed[u]:
            handle.wait_recv()
        weights[u] += [
            send_weights(u, 4, rows_at(base(left), half), to_right),
            send_weights(u, 5, rows_at(base(right) + half, half), to_left),
        ]
        if units[u][3] == "y":
            passed[u] = [
                send_weights(u, 6 + n, rows_at(base(x), OWNED), to_mate) for n, x in enumerate((across, right, left))
            ]
        else:
            passed[u] = []

    def pass_last(u):
        for handle in weights[u]:
            handle.wait_recv()
        base, _ = layout("y")
        passed[u].append(send_weights(u, 9, rows_at(base(opposite), OWNED), to_mate))

    def gathered(u):
        for handle in passed[u] if units[u][3] == "y" else weights[u]:
            handle.wait_recv()

    rescale_a(0)
    rescale_b(0)
    correlate(0, 0)
    a_near[1].wait_recv()
    rescale_a(1)
    correlate(0, 1)
    send_along_x(0)
    a_near[2].wait_recv()
    a_far = start(a_raw.at[2], a_raw.at[3], a_s.at[3], a_r.at[3], j_peer[1])
    b_far = []
    for r, first in ((1, 0), (3, ROWS // 2)):
        b_near[r].wait_recv()
        half = pl.ds(first, ROWS // 2)
        n = 2 if r == 1 else 0
        b_far.append(start(b_raw.at[r, half], b_raw.at[2, half], b_s.at[n], b_r.at[n], z_peer[4 - r]))
    relay(0)
    rescale_a(2)
    rescale_b(1)
    rescale_b(3)
    for k in (1, 3):
        for m in range(3):
            correlate(k, m)
    a_far.wait_recv()
    rescale_a(3)
    correlate(3, 3)
    cross(2)
    correlate(1, 3)
    send_along_x(1)
    correlate(0, 2)
    correlate(0, 3)
    cross(4)
    half_a = half_of(va, center_a, inverse_a)
    half_b = half_of(vb, center_b, inverse_b)
    shared_a = a_buf[0, 0:ROWS].astype(F32)
    shared_b = b_buf[0, 0:ROWS].astype(F32)
    mid[0] = jnp.concatenate(
        [column_sum(t) for t in (half_a * half_b, shared_a, shared_b, half_a, half_b)] + [zero_row] * 3, axis=0
    )
    mid_arrive = [start(mid.at[0], mid.at[r], mid_s.at[r], mid_r.at[r], dp_peer[r]) for r in range(1, 8)]
    cross_done(2)
    relay(1)
    for handle in b_far:
        handle.wait_recv()
    rescale_b(2)
    for m in range(4):
        correlate(2, m)
    send_along_x(3)
    cross_done(4)
    relay(2)
    reduce_x(1)
    for handle in mid_arrive:
        handle.wait_recv()
    totals = tree_sum([mid[r] for r in range(8)])
    sums_a[0] = totals
    sums_b[0] = totals
    sum_arrive = [start(sums_a.at[0], sums_a.at[r], sum_s.at[r], sum_r.at[r], j_peer[r]) for r in range(1, 4)]
    sum_arrive += [start(sums_b.at[0], sums_b.at[r], sum_s.at[3 + r], sum_r.at[3 + r], z_peer[r]) for r in range(1, 4)]
    diagonal = totals[0:1] / BATCH
    diag_weight = (-2.0 * (1.0 - diagonal)).astype(BF16).astype(F32)
    relay(3)
    reduce_done(1)
    reduce_x(0)
    relay(4)
    reduce_done(2)
    pass_mate(1)
    reduce_x(3)
    pass_far(2)
    reduce_done(4)
    reduce_done(0)
    pass_far(1)
    reduce_done(3)
    pass_last(2)
    pass_far(4)
    for handle in sum_arrive:
        handle.wait_recv()
    for r in range(4):
        for sums_ref, row, buf in ((sums_a, 1, a_buf), (sums_b, 2, b_buf)):
            value = sums_ref[r, row : row + 1]
            high = value.astype(BF16)
            low = (value - high.astype(F32)).astype(BF16)
            buf[r, ROWS : ROWS + EXTRA] = jnp.concatenate(
                [high.astype(F32), low.astype(F32), jnp.zeros((EXTRA - 2, COLS), F32)], axis=0
            ).astype(BF16)
    pass_mate(3)
    pass_mate(0)

    ub_arrive = {}
    vecb_arrive = {}
    ua_done = set()

    def squares(k):
        square = jnp.square(w_buf[k].astype(F32))
        if ua_done:
            second_acc[0:1] += column_sum(square)
        else:
            second_acc[0:1] = column_sum(square)
        folded = sum(square[:, i * 128 : (i + 1) * 128] for i in range(8))
        return column_sum(folded.T)

    def upstream_of_b(k, over_first):
        total = None
        for m in range(4):
            term = matmul(a_buf[m], w_buf[k, :, m * COLS : (m + 1) * COLS], ((1,), (1,)))
            total = term if total is None else total + term
        first = total[ROWS : ROWS + 1] + total[ROWS + 1 : ROWS + 2]
        slot = vec_b.at[0 if k == 0 else 3 + k]
        slot[...] = jnp.concatenate([first, over_first] + [zero_row] * 6, axis=0)
        if k:
            vecb_arrive[k] = start(slot, vec_b.at[k], vec_s.at[3 + k], vec_r.at[3 + k], z_peer[k])
        if k == 0:
            ub_own[...] = total[0:ROWS]
        else:
            ub_send[k] = (total[0:ROWS] - b_buf[k, 0:ROWS].astype(F32) * (over_first * along)).astype(BF16)
            ub_arrive[k] = start(ub_send.at[k], ub_recv.at[k], ub_s.at[k], ub_r.at[k], z_peer[k])

    def upstream_of_a(k, m):
        term = matmul(b_buf[k], w_buf[k, :, m * COLS : (m + 1) * COLS], ((1,), (0,)))
        if m in ua_done:
            ua_acc[m] += term
        else:
            ua_acc[m] = term
            ua_done.add(m)

    def take_out(r):
        taken = second_acc[0:1, r * COLS : (r + 1) * COLS] * along
        ua_acc[r, 0:ROWS] -= a_buf[r, 0:ROWS].astype(F32) * taken

    gathered(1)
    over_first = squares(1)
    upstream_of_b(1, over_first)
    for m in range(4):
        upstream_of_a(1, m)
    pass_far(3)
    pass_far(0)
    pass_last(4)
    gathered(2)
    over_first = squares(3)
    upstream_of_b(3, over_first)
    for m in range(4):
        upstream_of_a(3, m)
    gathered(3)
    over_first = squares(2)
    upstream_of_b(2, over_first)
    for m in range(4):
        upstream_of_a(2, m)
    gathered(0)
    gathered(4)
    over_first = squares(0)
    for m in (3, 1, 2, 0):
        upstream_of_a(0, m)
        if m == 3:
            take_out(3)
            ua3 = start(ua_acc.at[3, pl.ds(0, ROWS)], ua_near.at[1], ua_s.at[3], ua_r.at[3], j_peer[1])
    ua1 = start(ua_acc.at[1, pl.ds(0, ROWS)], ua_near.at[0], ua_s.at[1], ua_r.at[1], j_peer[1])
    take_out(2)

    block_sum = sum(second_acc[0:1, m * COLS : (m + 1) * COLS] for m in range(4))
    loss_row = (1.0 - diagonal) ** 2 + (0.25 / off_weight) * block_sum
    vec_arrive = []
    for r in range(4):
        first = ua_acc[r, ROWS : ROWS + 1] + ua_acc[r, ROWS + 1 : ROWS + 2]
        second = second_acc[0:1, r * COLS : (r + 1) * COLS]
        slot = vec_a.at[0 if r == 0 else 3 + r]
        slot[...] = jnp.concatenate([first, second, loss_row] + [zero_row] * 5, axis=0)
        if r:
            vec_arrive.append(start(slot, vec_a.at[r], vec_s.at[r], vec_r.at[r], j_peer[r]))
    ua3.wait_recv()
    ua_send[...] = (ua_acc[2, 0:ROWS] + ua_near[1]).astype(BF16)
    ua2 = start(ua_send, ua_recv, ua_s.at[2], ua_r.at[2], j_peer[2])
    upstream_of_b(0, over_first)
    for handle in vec_arrive:
        handle.wait_recv()
    sum_a = tree_sum([vec_a[r] for r in range(4)])
    vec_l[0] = sum_a
    loss_arrive = [start(vec_l.at[0], vec_l.at[r], vl_s.at[r], vl_r.at[r], z_peer[r]) for r in range(1, 4)]
    for handle in vecb_arrive.values():
        handle.wait_recv()
    sum_b = tree_sum([vec_b[r] for r in range(4)])
    def finish(upstream, view, center, inverse, own_sum, sums, out):
        first = (sums[0:1] + diag_weight * own_sum) / BATCH
        second = sums[1:2] * along + diag_weight * diagonal
        normed = (view[...] - center) * inverse
        out[...] = (upstream - first - normed * second) * inverse

    ua1.wait_recv()
    taken = (vec_a[2, 1:2] + vec_a[3, 1:2]) * along
    upstream_a = ua_acc[0, 0:ROWS] + ua_near[0] + diag_weight * half_of(vb, center_b, inverse_b)
    upstream_a = upstream_a + taken * a_buf[0, 0:ROWS].astype(F32)
    finish(upstream_a, va, center_a, inverse_a, totals[4:5], sum_a, ga)
    upstream_b = ub_own[...] + diag_weight * half_of(va, center_a, inverse_a)
    taken = (vec_b[1, 1:2] + vec_b[2, 1:2] + vec_b[3, 1:2]) * along
    upstream_b = upstream_b + taken * b_buf[0, 0:ROWS].astype(F32)
    finish(upstream_b, vb, center_b, inverse_b, totals[3:4], sum_b, gb)
    for k in (1, 3, 2):
        ub_arrive[k].wait_recv()
    gb[...] += sum(ub_recv[k].astype(F32) for k in (1, 2, 3)) * inverse_b
    for handle in loss_arrive:
        handle.wait_recv()
    losses = tree_sum([vec_l[r] for r in range(4)])
    loss[...] = jnp.sum(losses[2:3], axis=1, keepdims=True) / D
    for handle in pending:
        if handle is not ua2:
            handle.wait_send()
    ua2.wait_recv()
    ga[...] += ua_recv[...].astype(F32) * inverse_a
    ua2.wait_send()


def per_device(view_a, view_b):
    view = VMEM((ROWS, COLS), F32)
    small = VMEM((8, 8, COLS), F32)
    block = VMEM((4, ROWS + EXTRA, COLS), BF16)
    plain = VMEM((4, ROWS, COLS), BF16)
    chunk = (4, COLS, WIDE)
    pair = VMEM((4, 2 * OWNED, WIDE), BF16)
    grad_a, grad_b, loss = pl.pallas_call(
        kernel,
        out_shape=(
            jax.ShapeDtypeStruct((ROWS, COLS), F32),
            jax.ShapeDtypeStruct((ROWS, COLS), F32),
            jax.ShapeDtypeStruct((1, 1), F32),
        ),
        in_specs=[pl.BlockSpec(memory_space=pltpu.HBM)] * 2,
        out_specs=[pl.BlockSpec(memory_space=VMEM)] * 3,
        scratch_shapes=[
            view, view, small, small, small, small, small, small, small,
            VMEM((4, 8, COLS), F32), VMEM((4, 8, COLS), F32), plain, plain, block, block, VMEM((4, COLS, ROWS), BF16), VMEM(chunk, F32), VMEM(chunk, BF16), pair, pair, pair, VMEM((4, 4 * OWNED, WIDE), BF16),
            VMEM(chunk, BF16),
            VMEM((4, ROWS + EXTRA, COLS), F32), VMEM((ROWS, COLS), F32),
            VMEM((2, ROWS, COLS), F32), VMEM((ROWS, COLS), BF16), VMEM((ROWS, COLS), BF16), plain, plain, VMEM((8, WIDE), F32),
            DMA((2,)), *[DMA((8,))] * 12, *[DMA((4,))] * 4, *[DMA((5, 10))] * 4, *[DMA((4,))] * 4,
        ],
        compiler_params=pltpu.CompilerParams(
            collective_id=0, has_side_effects=True, vmem_limit_bytes=44 * 1024 * 1024
        ),
        cost_estimate=pl.CostEstimate(flops=3 * 2 * 1024**3, bytes_accessed=4 * 1024 * 1024, transcendentals=0),
        name="twins",
    )(view_a, view_b)
    return grad_a, grad_b, loss[0, 0]


def solution(mesh):
    in_specs = (P("dp", "feat"), P("dp", "feat"))
    out_specs = (P("dp", "feat"), P("dp", "feat"), P())
    return jax.shard_map(
        per_device, mesh=mesh, in_specs=in_specs, out_specs=out_specs, check_vma=False
    )
```
